32 devices in a mesh: group: 1, wide: 16 (over z, y, x), narrow: 2 (over core).
Axes of the slice: x: 2, y: 2, z: 4, core: 2. Of those that a mesh axis runs over, the one named last changes fastest.
Arguments:
- tokens: bfloat16 [256, 7168], P(('group', 'wide', 'narrow')), may hold values from -6 to 6
- expert_ids: int32 [256, 8], P(('group', 'wide', 'narrow')), may hold values from 0 to 15, all different within a row; in each aligned block of 8 rows (0 to 7, 8 to 15, ...) at most 8 rows name the same one
- gate_weights: float32 [256, 8], P(('group', 'wide', 'narrow')), may hold values from 0.05 to 0.3
- w_gate: bfloat16 [32, 7168, 512], P(('wide', 'narrow')), may hold values from -0.0625 to 0.0625
- w_up: bfloat16 [32, 7168, 512], P(('wide', 'narrow')), may hold values from -0.0625 to 0.0625
- w_down: bfloat16 [32, 512, 7168], P(('wide', 'narrow')), may hold values from -0.1875 to 0.1875
Outputs:
- mixed: bfloat16 [256, 7168], P(('group', 'wide', 'narrow'))
The draws below stay inside these ranges and needn't reach their ends.
Inputs may be any that keep to these rules, and one draw needn't show every extreme that they name: `expert_ids`: each token names 8 different experts. Among the 8 tokens of one device no expert is named by more than 8 tokens, and in every draw some expert is named by exactly 8 tokens of some device.
All inputs are finite; a program needn't handle non-finite values.
Results may differ from the reference program's by a relative error of at most 0.0058.
Values may be sent and summed in bfloat16 or wider, within the bound.
No kernel may reach another device: no remote copies, remote signals or barrier semaphores. Data moves between devices by JAX's collectives and lax.ppermute only.
A program may use at most 128 MiB of HBM per device.

```python
import math
import jax
import jax.numpy as jnp
import numpy as np
from jax import lax

D = 7168
TOP = 8
FF = 1024
TOK_DEV = 8
SLICES = 2
FS = 512
EXPERTS = 16
TOKENS = 256
CAP = 8
N_WIDE = 16
N_NARROW = 2


def block_levels(own_key, shape, split, low, largest):
    def one(dim, shards_of):
        heights = jax.random.uniform(jax.random.fold_in(jax.random.fold_in(own_key, 6), dim), (shards_of,), jnp.float32, low / len(split), largest / len(split))
        return jnp.repeat(jnp.exp(heights), shape[dim] // shards_of).reshape((-1,) + (1,) * (len(shape) - dim - 1))

    gain = one(*split[0])
    for cut in split[1:]:
        gain = gain * one(*cut)
    return gain


def assign_block(key, own, number, rows, count, top, limit, lean):
    order = jax.random.permutation(key, count)
    heavy_load, ordinary = portions_of(count, rows * top, limit, lean, True), portions_of(count, rows * top, limit, lean, False)
    places = jnp.arange(count)

    def named(sizes, turn):
        used = int((sizes > 0).sum())
        fixed = max(1, used // 4)
        shifted = fixed + (places - fixed + turn * (used - fixed)) % max(1, count - fixed)
        return jnp.zeros((count,), jnp.int32).at[order[jnp.where(places < fixed, places, shifted)]].set(jnp.asarray(sizes, jnp.int32))

    sizes = jnp.where(number % 4 == 0, named(heavy_load, number // 4), named(ordinary, number - number // 4 - 1))
    mixed = jax.random.permutation(jax.random.fold_in(own, 3), count)
    source_of, sink = mixed[0:count // 2 * 2:2], mixed[1:count // 2 * 2:2]
    room = jnp.minimum(sizes[source_of] - 1, limit - sizes[sink]) // 2
    room = jnp.where((source_of == order[0]) | (sink == order[0]) | (sizes[sink] == 0), 0, jnp.maximum(room, 0))
    shifted = jax.random.randint(jax.random.fold_in(own, 4), (count // 2,), 0, 1 << 20) % (room + 1)
    sizes = sizes.at[source_of].add(-shifted).at[sink].add(shifted)
    labels = jnp.searchsorted(jnp.cumsum(sizes), jnp.arange(rows * top), side="right").astype(jnp.int32)
    table = labels.reshape(top, rows).T
    table = table[jax.random.permutation(jax.random.fold_in(own, 1), rows)]
    turn = jax.random.randint(jax.random.fold_in(own, 2), (rows, 1), 0, top)
    return jnp.take_along_axis(table, (jnp.arange(top)[None, :] + turn) % top, axis=1)


def portions_of(number_of, total, limit, slope, full):
    portions = [(1 << 20) // math.isqrt(standing ** slope) + 1 for standing in range(1, number_of + 1)]
    largest = limit if full else min(limit, max(-(-total // number_of), total * portions[0] // sum(portions)))
    least = 1 if total - largest >= number_of - 1 else 0
    given, spare = [largest] + [least] * (number_of - 1), total - largest - least * (number_of - 1)
    while spare > 0:
        free = [i for i in range(1, number_of) if given[i] < largest] or [i for i in range(1, number_of) if given[i] < limit]
        pool, budget = sum([portions[i] for i in free]), spare
        for i in free:
            extra = min(limit - given[i], max(1, budget * portions[i] // pool), spare)
            given[i] = given[i] + extra
            spare = spare - extra
    return np.array(given)


def bell_draw(stream_key, extent, scale, most, pieces=(), held_as=jnp.bfloat16):
    entries = jax.random.normal(stream_key, extent, jnp.float32) * scale
    if len(pieces) > 0:
        entries = block_levels(stream_key, extent, pieces, -0.22, 0.18) * entries
    return jnp.clip(entries, min=-most, max=most).astype(held_as)


def setup_inputs(seed: int = 0, part: int = 0) -> dict:
    keys = jax.random.split(jax.random.key(seed), 7)
    own_keys = jax.random.split(jax.random.fold_in(keys[6], part), 7)
    tokens = bell_draw(own_keys[0], (TOKENS, D), 1.0, 6.0, ((0, 32),))
    expert_ids_keys = jax.random.split(jax.random.fold_in(own_keys[1], 1), TOKENS // TOK_DEV)
    expert_ids_turns = jax.random.permutation(jax.random.fold_in(own_keys[1], 3), TOKENS // TOK_DEV)
    expert_ids = jax.vmap(lambda own, number: assign_block(jax.random.fold_in(own_keys[1], 2), own, number, TOK_DEV, EXPERTS, TOP, CAP, 2))(expert_ids_keys, expert_ids_turns).reshape((TOKENS, TOP))
    gate_weights = jnp.clip(0.05 + 0.25 * jax.random.uniform(own_keys[2], (TOKENS, TOP), jnp.float32) ** block_levels(own_keys[2], (TOKENS, TOP), ((0, 32),), -0.2, 0.2), 0.05, 0.3)
    w_gate = bell_draw(keys[3], (EXPERTS * SLICES, D, FS), D ** -0.5, 0.0625, ((0, 32),))
    w_up = bell_draw(keys[4], (EXPERTS * SLICES, D, FS), D ** -0.5, 0.0625, ((0, 32),))
    w_down = bell_draw(keys[5], (EXPERTS * SLICES, FS, D), FF ** -0.5, 0.1875, ((0, 32),))
    return {"tokens": tokens, "expert_ids": expert_ids, "gate_weights": gate_weights, "w_gate": w_gate, "w_up": w_up, "w_down": w_down}


def reference(tokens, expert_ids, gate_weights, w_gate, w_up, w_down):
    tokens_all, width = tokens.shape
    routed = tokens_all * TOP
    flat_ids = expert_ids.reshape(routed).astype(jnp.int32)
    order = jnp.argsort(flat_ids, stable=True).astype(jnp.int32)
    sorted_ids = flat_ids[order]
    counts = jnp.sum((flat_ids[:, None] == jnp.arange(EXPERTS, dtype=jnp.int32)[None, :]).astype(jnp.int32), 0)
    starts = (jnp.cumsum(counts) - counts).astype(jnp.int32)
    span = N_WIDE * N_NARROW * CAP
    copies = tokens[order // TOP]
    padded = jnp.concatenate([copies, jnp.zeros((span, width), tokens.dtype)], 0)
    gate_all = w_gate.reshape(EXPERTS, SLICES, width, FS)
    up_all = w_up.reshape(EXPERTS, SLICES, width, FS)
    down_all = w_down.reshape(EXPERTS, SLICES, FS, width)

    def one_expert(expert):
        rows = lax.dynamic_slice_in_dim(padded, starts[expert], span, 0)
        total = jnp.zeros((span, width), jnp.float32)
        for piece in range(SLICES):
            gate = jnp.dot(rows, gate_all[expert, piece], preferred_element_type=jnp.float32)
            up = jnp.dot(rows, up_all[expert, piece], preferred_element_type=jnp.float32)
            hidden = (jax.nn.silu(gate) * up).astype(jnp.bfloat16)
            partial_out = jnp.dot(hidden, down_all[expert, piece], preferred_element_type=jnp.float32).astype(jnp.bfloat16)
            total = total + partial_out.astype(jnp.float32)
        return total

    outputs = lax.map(one_expert, jnp.arange(EXPERTS, dtype=jnp.int32))
    position = jnp.arange(routed, dtype=jnp.int32) - starts[sorted_ids]
    sorted_out = outputs.reshape(EXPERTS * span, width)[sorted_ids * span + position]
    result = jnp.zeros((routed, width), jnp.float32).at[order].set(sorted_out)
    picked = result.reshape(tokens_all, TOP, width)
    mixed = jnp.sum(picked * gate_weights.astype(jnp.float32)[:, :, None], 1)
    return mixed.astype(jnp.bfloat16)
```

```python
import jax
import jax.numpy as jnp
from jax import lax
from jax.sharding import PartitionSpec as P

FF = 1024
AXES = ("wide", "narrow")
LANES = 128
F32 = jnp.float32
BF16 = jnp.bfloat16


def exchanges(n_wide, n_narrow):
    n = n_wide * n_narrow
    inner = min(4, n_wide)
    steps = []
    stride = inner * n_narrow
    rest = n_wide // inner
    while rest > 1:
        radix = min(4, rest)
        steps.append([[(i, i ^ (k * stride)) for i in range(n)] for k in range(1, radix)])
        stride *= radix
        rest //= radix
    if inner == 4:
        a, b = n_narrow, 2 * n_narrow
        steps.append([[(i, i ^ (a if i % n_narrow == 0 else b)) for i in range(n)]])
        steps.append([[(i, i ^ (b if i % n_narrow == 0 else a)) for i in range(n)]])
    elif inner == 2:
        steps.append([[(i, i ^ n_narrow) for i in range(n)]])
    if n_narrow == 2:
        steps.append([[(i, i ^ 1) for i in range(n)]])
    return steps


def gather(block, steps):
    for step in steps:
        block = jnp.concatenate([block] + [lax.ppermute(block, AXES, p) for p in step], 0)
    return block


def scatter_sum(share, steps):
    for step in reversed(steps):
        rows = share.shape[0] // (len(step) + 1)
        got = [lax.ppermute(share[(k + 1) * rows:(k + 2) * rows].astype(BF16), AXES, p) for k, p in enumerate(step)]
        share = share[:rows]
        for g in got:
            share = share + g.astype(F32)
    return share


def split3(v):
    high = lax.reduce_precision(v, 8, 7)
    mid = lax.reduce_precision(v - high, 8, 7)
    low = lax.reduce_precision(v - high - mid, 8, 7)
    return [high, mid, low]


def body(tokens, expert_ids, gate_weights, w_gate, w_up, w_down):
    n_wide = lax.axis_size("wide")
    n_narrow = lax.axis_size("narrow")
    slices = FF // w_gate.shape[2]
    experts = n_wide * n_narrow // slices
    expert = lax.axis_index(AXES) // slices
    rows, width = tokens.shape
    steps = exchanges(n_wide, n_narrow)

    named = expert_ids[:, :, None] == jnp.arange(experts, dtype=jnp.int32)[None, None, :]
    table = jnp.sum(jnp.where(named, gate_weights[:, :, None], 0.0), 1)
    extra = jnp.concatenate(split3(table) + [jnp.zeros((rows, LANES - 3 * experts), F32)], 1).astype(BF16)
    sent = jnp.concatenate([tokens, extra], 1)

    cut = width // 2 // LANES * LANES
    first = gather(sent[:, :cut], steps)
    second = gather(sent[:, cut:], steps)
    lane = jnp.arange(LANES, dtype=jnp.int32)
    mine = (lane % experts == expert) & (lane < 3 * experts)
    scale = jnp.sum(jnp.where(mine[None, :], second[:, width - cut:].astype(F32), 0.0), 1, keepdims=True)
    second = second[:, :width - cut]

    def dot(a, b):
        return jnp.dot(a, b, preferred_element_type=F32)

    gate = dot(first, w_gate[0, :cut]) + dot(second, w_gate[0, cut:])
    up = dot(first, w_up[0, :cut]) + dot(second, w_up[0, cut:])
    hidden = (jax.nn.silu(gate) * up).astype(BF16)
    outs = []
    for a, b in ((0, cut), (cut, width)):
        share = dot(hidden, w_down[0, :, a:b]) * scale
        outs.append(scatter_sum(share, steps).astype(BF16))
    return jnp.concatenate(outs, 1)


def solution(mesh):
    in_specs = (
        P(("group", "wide", "narrow"), None),
        P(("group", "wide", "narrow"), None),
        P(("group", "wide", "narrow"), None),
        P(("wide", "narrow"), None, None),
        P(("wide", "narrow"), None, None),
        P(("wide", "narrow"), None, None),
    )
    out_specs = P(("group", "wide", "narrow"), None)
    return jax.shard_map(body, mesh=mesh, in_specs=in_specs, out_specs=out_specs, check_vma=False)
```

```python
import functools

import jax
import jax.numpy as jnp
from jax import lax
from jax.experimental import pallas as pl
from jax.experimental.pallas import tpu as pltpu
from jax.sharding import PartitionSpec as P

FF = 1024
AXES = ("wide", "narrow")
LANES = 128
CUT = 7
DOWN = 7
TIE = 0
F32 = jnp.float32
BF16 = jnp.bfloat16


def exchanges(n_wide):
    n = 2 * n_wide
    steps = []
    stride = 8
    rest = n_wide // 4
    while rest > 1:
        radix = min(4, rest)
        steps.append([[(i, i ^ (k * stride)) for i in range(n)] for k in range(1, radix)])
        stride *= radix
        rest //= radix
    steps.append([[(i, i ^ (2 if i % 2 == 0 else 4)) for i in range(n)]])
    last = [(i, i ^ (4 if i % 2 == 0 else 2)) for i in range(n)]
    core = [(i, i ^ 1) for i in range(n)]
    return steps, last, core


def move(x, perm):
    return lax.ppermute(x, AXES, perm)


def after(x, y):
    return lax.optimization_barrier((x, y))


def gather(block, cut, first_product, plan):
    steps, last, core = plan
    for step in steps[:-2]:
        block = jnp.concatenate([block] + [move(block, p) for p in step], 0)
    blocks = [block] + [move(block, p) for p in steps[-2]]
    one, two = [jnp.concatenate([x[:, at] for x in blocks], 0) for at in (slice(0, cut), slice(cut, None))]
    one, two = [jnp.concatenate([x, move(x, steps[-1][0])], 0) for x in (one, two)]
    other = move(one, last)
    acc = first_product((one, other, move(one, core), move(other, core)))
    other = move(two, last)
    return acc, (two, other, move(two, core), move(other, core))


def scatter_sum(near, near_sent, far, plan):
    steps, last, core = plan
    share = near + move(near_sent, core).astype(F32)
    share = share + move(far, last).astype(F32)
    for step in reversed(steps):
        rows = share.shape[0] // (len(step) + 1)
        got = [move(share[(k + 1) * rows:(k + 2) * rows].astype(BF16), p) for k, p in enumerate(step)]
        share = share[:rows]
        for g in got:
            share = share + g.astype(F32)
    return share


def split3(v):
    high = lax.reduce_precision(v, 8, 7)
    mid = lax.reduce_precision(v - high, 8, 7)
    low = lax.reduce_precision(v - high - mid, 8, 7)
    return [high, mid, low]


def dot(a, b):
    return jnp.dot(a, b, preferred_element_type=F32)


class Stream:
    def __init__(self, groups, ahead):
        self.groups, self.ahead, self.used = groups, ahead, 0
        for group in groups[:ahead]:
            for c in group:
                c.start()

    def wait(self):
        for c in self.groups[self.used]:
            c.wait()
        self.used += 1
        after = self.used + self.ahead - 1
        if after < len(self.groups):
            for c in self.groups[after]:
                c.start()


def up_copies(skip, kb, count, wg, wu, wg_held, wu_held, sems):
    groups = []
    for j in range(count):
        at, to = pl.ds(skip + j * kb, kb), pl.ds(j * kb, kb)
        groups.append([
            pltpu.make_async_copy(wg.at[0, at], wg_held.at[to], sems.at[0, j]),
            pltpu.make_async_copy(wu.at[0, at], wu_held.at[to], sems.at[1, j]),
        ])
    return groups


def down_copies(skip, cb, count, wd, held, sems):
    return [[pltpu.make_async_copy(wd.at[0, :, pl.ds(skip + j * cb, cb)], held.at[j], sems.at[j])] for j in range(count)]


def first_kernel(skip, kb, x0, x1, x2, x3, wg, wu, acc, rows, wg_held, wu_held, sems):
    q, width = x0.shape
    hid = wg.shape[2]
    count = width // kb
    stream = Stream(up_copies(skip, kb, count, wg, wu, wg_held, wu_held, sems), 4)
    for j in range(count):
        for n, x in enumerate((x0, x1, x2, x3)):
            rows[n * q:(n + 1) * q, :] = x[:, j * kb:(j + 1) * kb]
        stream.wait()
        gate = dot(rows[...], wg_held[j * kb:(j + 1) * kb, :])
        up = dot(rows[...], wu_held[j * kb:(j + 1) * kb, :])
        if j == 0:
            acc[:, :hid] = gate
            acc[:, hid:] = up
        else:
            acc[:, :hid] += gate
            acc[:, hid:] += up


def second_kernel(skip, kb, x0, x1, x2, x3, mask, acc, wg, wu, wd, hidden, scale, near, far, near_sent, far_sent,
                  rows, total, wg_held, wu_held, sems, wd_held, wd_sems):
    q = x0.shape[0]
    hid = wg.shape[2]
    width = x0.shape[1] - LANES
    count = width // kb
    stream = Stream(
        up_copies(skip, kb, count, wg, wu, wg_held, wu_held, sems)
        + down_copies(0, kb, near.shape[1] // kb, wd, wd_held, wd_sems),
        5,
    )
    for n, x in enumerate((x0, x1, x2, x3)):
        s = jnp.sum(x[:, width:].astype(F32) * mask[...], 1, keepdims=True)
        scale[n * q:(n + 1) * q, :] = jnp.broadcast_to(s, (q, LANES))
    for j in range(count):
        for n, x in enumerate((x0, x1, x2, x3)):
            rows[n * q:(n + 1) * q, :] = x[:, j * kb:(j + 1) * kb]
        stream.wait()
        held = acc if j == 0 else total
        gate = held[:, :hid] + dot(rows[...], wg_held[j * kb:(j + 1) * kb, :])
        up = held[:, hid:] + dot(rows[...], wu_held[j * kb:(j + 1) * kb, :])
        if j < count - 1:
            total[:, :hid] = gate
            total[:, hid:] = up
        else:
            hidden[...] = (gate / (1 + jnp.exp(-gate)) * up).astype(BF16)
    down_blocks(stream, kb, hidden, scale, wd_held, near, far, near_sent, far_sent)


def down_blocks(stream, cb, hidden, scale, held, near, far, near_sent, far_sent):
    q = near.shape[0]
    for j in range(near.shape[1] // cb):
        at = slice(j * cb, (j + 1) * cb)
        stream.wait()
        share = dot(hidden[...], held[j]) * scale[:, :1]
        near[:, at] = share[:q]
        far[:, at] = share[q:2 * q]
        near_sent[:, at] = share[2 * q:3 * q].astype(BF16)
        far_sent[:, at] = share[3 * q:].astype(BF16)


def down_kernel(skip, cb, hidden, scale, wd, near, far, near_sent, far_sent, held, sems):
    stream = Stream(down_copies(skip, cb, near.shape[1] // cb, wd, held, sems), 99)
    down_blocks(stream, cb, hidden, scale, held, near, far, near_sent, far_sent)


def in_vmem(n):
    return [pl.BlockSpec(memory_space=pltpu.VMEM)] * n


def in_hbm(n):
    return [pl.BlockSpec(memory_space=pltpu.HBM)] * n


def params(mib):
    return pltpu.CompilerParams(vmem_limit_bytes=mib << 20)


def first_part(pieces, w_gate, w_up, width, kb):
    q = pieces[0].shape[0]
    hid = w_gate.shape[2]
    return pl.pallas_call(
        functools.partial(first_kernel, 0, kb),
        in_specs=in_vmem(4) + in_hbm(2),
        out_specs=in_vmem(1)[0],
        out_shape=jax.ShapeDtypeStruct((4 * q, 2 * hid), F32),
        scratch_shapes=[pltpu.VMEM((4 * q, kb), BF16)] + held_up(width, hid, kb),
        compiler_params=params(30),
        cost_estimate=cost(16 * q * width * hid, 4 * width * hid),
    )(*pieces, w_gate, w_up)


def second_part(pieces, mask, acc, w_gate, w_up, w_down, skip, width, first, kb):
    q = pieces[0].shape[0]
    hid = w_gate.shape[2]
    return pl.pallas_call(
        functools.partial(second_kernel, skip, kb),
        in_specs=in_vmem(6) + in_hbm(3),
        out_specs=in_vmem(6),
        out_shape=[jax.ShapeDtypeStruct((4 * q, hid), BF16), jax.ShapeDtypeStruct((4 * q, LANES), F32)] + shares(q, first),
        scratch_shapes=[pltpu.VMEM((4 * q, kb), BF16), pltpu.VMEM((4 * q, 2 * hid), F32)]
        + held_up(width, hid, kb) + held_down(first, hid, kb),
        compiler_params=params(30),
        cost_estimate=cost(16 * q * width * hid + 8 * q * first * hid, 4 * width * hid + 2 * first * hid),
    )(*pieces, mask, acc, w_gate, w_up, w_down)


def down_part(hidden, scale, w_down, skip, width, kb):
    q = hidden.shape[0] // 4
    hid = hidden.shape[1]
    return pl.pallas_call(
        functools.partial(down_kernel, skip, kb),
        in_specs=in_vmem(2) + in_hbm(1),
        out_specs=in_vmem(4),
        out_shape=shares(q, width),
        scratch_shapes=held_down(width, hid, kb),
        compiler_params=params(20),
        cost_estimate=cost(8 * q * width * hid, 2 * width * hid),
    )(hidden, scale, w_down)


def cost(flops, moved):
    return pl.CostEstimate(flops=flops, bytes_accessed=moved, transcendentals=0)


def shares(q, width):
    return [jax.ShapeDtypeStruct((q, width), t) for t in (F32, F32, BF16, BF16)]


def held_up(width, hid, kb):
    return [pltpu.VMEM((width, hid), BF16)] * 2 + [pltpu.SemaphoreType.DMA((2, width // kb))]


def held_down(width, hid, kb):
    return [pltpu.VMEM((width // kb, hid, kb), BF16), pltpu.SemaphoreType.DMA((width // kb,))]


def body(tokens, expert_ids, gate_weights, w_gate, w_up, w_down):
    n_wide = lax.axis_size("wide")
    slices = FF // w_gate.shape[2]
    experts = 2 * n_wide // slices
    expert = lax.axis_index(AXES) // slices
    rows, width = tokens.shape
    plan = exchanges(n_wide)

    named = expert_ids[:, :, None] == jnp.arange(experts, dtype=jnp.int32)[None, None, :]
    table = jnp.sum(jnp.where(named, gate_weights[:, :, None], 0.0), 1)
    extra = jnp.concatenate(split3(table) + [jnp.zeros((rows, LANES - 3 * experts), F32)], 1).astype(BF16)
    lane = jnp.arange(LANES, dtype=jnp.int32)
    mask = ((lane % experts == expert) & (lane < 3 * experts)).astype(F32)[None, :]

    w_gate, w_up, w_down = [pltpu.with_memory_space_constraint(w, pltpu.HBM) for w in (w_gate, w_up, w_down)]
    kb = 512
    cut = CUT * width // kb // 14 * kb
    down = DOWN * width // kb // 14 * kb
    sent = jnp.concatenate([tokens, extra], 1)
    acc, two = gather(sent, cut, lambda one: first_part(one, w_gate, w_up, cut, kb), plan)
    hidden, scale, *pieces = second_part(two, mask, acc, w_gate, w_up, w_down, cut, width - cut, down, kb)
    far = pieces[1] + move(pieces[3], plan[2]).astype(F32)
    far = far.astype(BF16)
    if TIE:
        far, hidden = after(far, hidden)
    out = scatter_sum(pieces[0], pieces[2], far, plan)
    pieces = down_part(hidden, scale, w_down, down, width - down, kb)
    far = pieces[1] + move(pieces[3], plan[2]).astype(F32)
    rest = scatter_sum(pieces[0], pieces[2], far.astype(BF16), plan)
    return jnp.concatenate([out.astype(BF16), rest.astype(BF16)], 1)


def solution(mesh):
    tokens = P(("group", "wide", "narrow"), None)
    weights = P(("wide", "narrow"), None, None)
    return jax.shard_map(body, mesh=mesh, in_specs=(tokens,) * 3 + (weights,) * 3, out_specs=tokens, check_vma=False)
```

```python
import functools

import jax
import jax.numpy as jnp
from jax import lax
from jax.experimental import pallas as pl
from jax.experimental.pallas import tpu as pltpu
from jax.sharding import PartitionSpec as P

FF = 1024
AXES = ("wide", "narrow")
LANES = 128
CUT = 7
DOWN = 7
AHEAD = 3
FIRST = 2
SECOND = 30
F32 = jnp.float32
BF16 = jnp.bfloat16


def exchanges(n_wide):
    n = 2 * n_wide
    steps = []
    stride = 8
    rest = n_wide // 4
    while rest > 1:
        radix = min(4, rest)
        steps.append([[(i, i ^ (k * stride)) for i in range(n)] for k in range(1, radix)])
        stride *= radix
        rest //= radix
    steps.append([[(i, i ^ (2 if i % 2 == 0 else 4)) for i in range(n)]])
    last = [(i, i ^ (4 if i % 2 == 0 else 2)) for i in range(n)]
    core = [(i, i ^ 1) for i in range(n)]
    return steps, last, core


def move(x, perm):
    return lax.ppermute(x, AXES, perm)


def after(x, y):
    return lax.optimization_barrier((x, y))


def gather(block, extra, cut, first_product, plan):
    steps, last, core = plan
    for step in steps[:-2]:
        block, extra = [jnp.concatenate([x] + [move(x, p) for p in step], 0) for x in (block, extra)]
    blocks = [block] + [move(block, p) for p in steps[-2]]
    extra, blocks[1] = after(extra, blocks[1])
    extras = [extra] + [move(extra, p) for p in steps[-2]]
    one = jnp.concatenate([x[:, :cut] for x in blocks], 0)
    two = jnp.concatenate([jnp.concatenate([x[:, cut:], e], 1) for x, e in zip(blocks, extras)], 0)
    one, two = [jnp.concatenate([x, move(x, steps[-1][0])], 0) for x in (one, two)]
    other = move(one, last)
    acc = first_product((one, other, move(one, core), move(other, core)))
    other = move(two, last)
    return acc, (two, other, move(two, core), move(other, core))


def scatter_sum(near, near_sent, far, plan):
    steps, last, core = plan
    share = near + move(near_sent, core).astype(F32)
    share = share + move(far, last).astype(F32)
    for step in reversed(steps):
        rows = share.shape[0] // (len(step) + 1)
        got = [move(share[(k + 1) * rows:(k + 2) * rows].astype(BF16), p) for k, p in enumerate(step)]
        share = share[:rows]
        for g in got:
            share = share + g.astype(F32)
    return share


def split3(v):
    high = lax.reduce_precision(v, 8, 7)
    mid = lax.reduce_precision(v - high, 8, 7)
    low = lax.reduce_precision(v - high - mid, 8, 7)
    return [high, mid, low]


def dot(a, b):
    return jnp.dot(a, b, preferred_element_type=F32)


class Stream:
    def __init__(self, groups, ahead):
        self.groups, self.ahead, self.used = groups, ahead, 0
        for group in groups[:ahead]:
            for c in group:
                c.start()

    def wait(self):
        for c in self.groups[self.used]:
            c.wait()
        self.used += 1
        after = self.used + self.ahead - 1
        if after < len(self.groups):
            for c in self.groups[after]:
                c.start()


def up_copies(skip, kb, count, wg, wu, wg_held, wu_held, sems):
    groups = []
    for j in range(count):
        at, to = pl.ds(skip + j * kb, kb), pl.ds(j * kb, kb)
        groups.append([
            pltpu.make_async_copy(wg.at[0, at], wg_held.at[to], sems.at[0, j]),
            pltpu.make_async_copy(wu.at[0, at], wu_held.at[to], sems.at[1, j]),
        ])
    return groups


def down_copies(skip, cb, count, wd, held, sems):
    return [[pltpu.make_async_copy(wd.at[0, :, pl.ds(skip + j * cb, cb)], held.at[j], sems.at[j])] for j in range(count)]


def first_kernel(skip, kb, x0, x1, x2, x3, wg, wu, acc, rows, wg_held, wu_held, sems):
    q, width = x0.shape
    hid = wg.shape[2]
    count = width // kb
    stream = Stream(up_copies(skip, kb, count, wg, wu, wg_held, wu_held, sems), FIRST)
    for j in range(count):
        for n, x in enumerate((x0, x1, x2, x3)):
            rows[n * q:(n + 1) * q, :] = x[:, j * kb:(j + 1) * kb]
        stream.wait()
        gate = dot(rows[...], wg_held[j * kb:(j + 1) * kb, :])
        up = dot(rows[...], wu_held[j * kb:(j + 1) * kb, :])
        if j == 0:
            acc[:, :hid] = gate
            acc[:, hid:] = up
        else:
            acc[:, :hid] += gate
            acc[:, hid:] += up


def second_kernel(skip, kb, x0, x1, x2, x3, mask, acc, wg, wu, wd, *rest):
    near, rest = rest[0:4], rest[4:]
    later, rest = rest[0:4], rest[4:]
    rows, total, hidden, scale, wg_held, wu_held, sems, wd_held, wd_sems = rest
    q = x0.shape[0]
    hid = wg.shape[2]
    width = x0.shape[1] - LANES
    count = width // kb
    stream = Stream(
        up_copies(skip, kb, count, wg, wu, wg_held, wu_held, sems)
        + down_copies(0, kb, wd_held.shape[0], wd, wd_held, wd_sems),
        AHEAD,
    )
    for n, x in enumerate((x0, x1, x2, x3)):
        s = jnp.sum(x[:, width:].astype(F32) * mask[...], 1, keepdims=True)
        scale[n * q:(n + 1) * q, :] = jnp.broadcast_to(s, (q, LANES))
    for j in range(count):
        for n, x in enumerate((x0, x1, x2, x3)):
            rows[n * q:(n + 1) * q, :] = x[:, j * kb:(j + 1) * kb]
        stream.wait()
        held = acc if j == 0 else total
        gate = held[:, :hid] + dot(rows[...], wg_held[j * kb:(j + 1) * kb, :])
        up = held[:, hid:] + dot(rows[...], wu_held[j * kb:(j + 1) * kb, :])
        if j < count - 1:
            total[:, :hid] = gate
            total[:, hid:] = up
        else:
            hidden[...] = (gate / (1 + jnp.exp(-gate)) * up).astype(BF16)
    down_blocks(stream, 0, hidden, scale, wd_held, *near)
    down_blocks(stream, near[0].shape[1] // kb, hidden, scale, wd_held, *later)


def down_blocks(stream, base, hidden, scale, held, near, far, near_sent, far_sent):
    q = near.shape[0]
    cb = held.shape[2]
    for j in range(near.shape[1] // cb):
        at = slice(j * cb, (j + 1) * cb)
        stream.wait()
        share = dot(hidden[...], held[base + j]) * scale[:, :1]
        near[:, at] = share[:q]
        far[:, at] = share[q:2 * q]
        near_sent[:, at] = share[2 * q:3 * q].astype(BF16)
        far_sent[:, at] = share[3 * q:].astype(BF16)


def in_vmem(n):
    return [pl.BlockSpec(memory_space=pltpu.VMEM)] * n


def in_hbm(n):
    return [pl.BlockSpec(memory_space=pltpu.HBM)] * n


def params(mib):
    return pltpu.CompilerParams(vmem_limit_bytes=mib << 20)


def first_part(pieces, w_gate, w_up, width, kb):
    q = pieces[0].shape[0]
    hid = w_gate.shape[2]
    return pl.pallas_call(
        functools.partial(first_kernel, 0, kb),
        in_specs=in_vmem(4) + in_hbm(2),
        out_specs=in_vmem(1)[0],
        out_shape=jax.ShapeDtypeStruct((4 * q, 2 * hid), F32),
        scratch_shapes=[pltpu.VMEM((4 * q, kb), BF16)] + held_up(width, hid, kb),
        compiler_params=params(30),
        cost_estimate=cost(16 * q * width * hid, 4 * width * hid),
    )(*pieces, w_gate, w_up)


def second_part(pieces, mask, acc, w_gate, w_up, w_down, skip, down, kb):
    q = pieces[0].shape[0]
    _, full, hid = w_gate.shape
    width = full - skip
    rows = 4 * q
    return pl.pallas_call(
        functools.partial(second_kernel, skip, kb),
        in_specs=in_vmem(6) + in_hbm(3),
        out_specs=in_vmem(8),
        out_shape=shares(q, down) + shares(q, full - down),
        scratch_shapes=[pltpu.VMEM((rows, kb), BF16), pltpu.VMEM((rows, 2 * hid), F32), pltpu.VMEM((rows, hid), BF16), pltpu.VMEM((rows, LANES), F32)]
        + held_up(width, hid, kb) + held_down(full, hid, kb),
        compiler_params=params(SECOND),
        cost_estimate=cost(4 * rows * width * hid + 2 * rows * full * hid, 4 * width * hid + 2 * full * hid),
    )(*pieces, mask, acc, w_gate, w_up, w_down)


def cost(flops, moved):
    return pl.CostEstimate(flops=flops, bytes_accessed=moved, transcendentals=0)


def shares(q, width):
    return [jax.ShapeDtypeStruct((q, width), t) for t in (F32, F32, BF16, BF16)]


def held_up(width, hid, kb):
    return [pltpu.VMEM((width, hid), BF16)] * 2 + [pltpu.SemaphoreType.DMA((2, width // kb))]


def held_down(width, hid, kb):
    return [pltpu.VMEM((width // kb, hid, kb), BF16), pltpu.SemaphoreType.DMA((width // kb,))]


def body(tokens, expert_ids, gate_weights, w_gate, w_up, w_down):
    n_wide = lax.axis_size("wide")
    slices = FF // w_gate.shape[2]
    experts = 2 * n_wide // slices
    expert = lax.axis_index(AXES) // slices
    rows, width = tokens.shape
    plan = exchanges(n_wide)

    named = expert_ids[:, :, None] == jnp.arange(experts, dtype=jnp.int32)[None, None, :]
    table = jnp.sum(jnp.where(named, gate_weights[:, :, None], 0.0), 1)
    extra = jnp.concatenate(split3(table) + [jnp.zeros((rows, LANES - 3 * experts), F32)], 1).astype(BF16)
    lane = jnp.arange(LANES, dtype=jnp.int32)
    mask = ((lane % experts == expert) & (lane < 3 * experts)).astype(F32)[None, :]

    w_gate, w_up, w_down = [pltpu.with_memory_space_constraint(w, pltpu.HBM) for w in (w_gate, w_up, w_down)]
    kb = width // (4 if rows * 2 * n_wide <= 256 else 14)
    cut = CUT * (width // kb) // 14 * kb
    down = DOWN * (width // kb) // 14 * kb
    acc, two = gather(tokens, extra, cut, lambda one: first_part(one, w_gate, w_up, cut, kb), plan)
    pieces = second_part(two, mask, acc, w_gate, w_up, w_down, cut, down, kb)
    core = plan[2]
    far = (pieces[1] + move(pieces[3], core).astype(F32)).astype(BF16)
    out = scatter_sum(pieces[0], pieces[2], far, plan)
    far = (pieces[5] + move(pieces[7], core).astype(F32)).astype(BF16)
    rest = scatter_sum(pieces[4], pieces[6], far, plan)
    return jnp.concatenate([out.astype(BF16), rest.astype(BF16)], 1)


def solution(mesh):
    tokens = P(("group", "wide", "narrow"), None)
    weights = P(("wide", "narrow"), None, None)
    return jax.shard_map(body, mesh=mesh, in_specs=(tokens,) * 3 + (weights,) * 3, out_specs=tokens, check_vma=False)
```

```python
import functools

import jax
import jax.numpy as jnp
from jax import lax
from jax.experimental import pallas as pl
from jax.experimental.pallas import tpu as pltpu
from jax.sharding import PartitionSpec as P

FF = 1024
AXES = ("wide", "narrow")
LANES = 128
CUT = 7
DOWN = 7
AHEAD = 3
FIRST = 2
SECOND = 30
WEIGHT = 20
F32 = jnp.float32
BF16 = jnp.bfloat16


def exchanges(n_wide):
    n = 2 * n_wide
    steps = []
    stride = 8
    rest = n_wide // 4
    while rest > 1:
        radix = min(4, rest)
        steps.append([[(i, i ^ (k * stride)) for i in range(n)] for k in range(1, radix)])
        stride *= radix
        rest //= radix
    steps.append([[(i, i ^ (2 if i % 2 == 0 else 4)) for i in range(n)]])
    last = [(i, i ^ (4 if i % 2 == 0 else 2)) for i in range(n)]
    core = [(i, i ^ 1) for i in range(n)]
    return steps, last, core


def move(x, perm):
    return lax.ppermute(x, AXES, perm)


def after(x, y):
    return lax.optimization_barrier((x, y))


def gather(block, extra, cut, first_product, plan):
    steps, last, core = plan
    for step in steps[:-2]:
        block, extra = [jnp.concatenate([x] + [move(x, p) for p in step], 0) for x in (block, extra)]
    blocks = [block] + [move(block, p) for p in steps[-2]]
    extra, blocks[1] = after(extra, blocks[1])
    extras = [extra] + [move(extra, p) for p in steps[-2]]
    one = jnp.concatenate([x[:, :cut] for x in blocks], 0)
    two = jnp.concatenate([jnp.concatenate([x[:, cut:], e], 1) for x, e in zip(blocks, extras)], 0)
    one, two = [jnp.concatenate([x, move(x, steps[-1][0])], 0) for x in (one, two)]
    other = move(one, last)
    acc = first_product((one, other, move(one, core), move(other, core)))
    other = move(two, last)
    return acc, (two, other, move(two, core), move(other, core))


def scatter_sum(near, near_sent, far, plan):
    steps, last, core = plan
    share = near + move(near_sent, core).astype(F32)
    share = share + move(far, last).astype(F32)
    for step in reversed(steps):
        rows = share.shape[0] // (len(step) + 1)
        got = [move(share[(k + 1) * rows:(k + 2) * rows].astype(BF16), p) for k, p in enumerate(step)]
        share = share[:rows]
        for g in got:
            share = share + g.astype(F32)
    return share


def split3(v):
    high = lax.reduce_precision(v, 8, 7)
    mid = lax.reduce_precision(v - high, 8, 7)
    low = lax.reduce_precision(v - high - mid, 8, 7)
    return [high, mid, low]


def dot(a, b):
    return jnp.dot(a, b, preferred_element_type=F32)


class Stream:
    def __init__(self, groups, ahead):
        self.groups, self.ahead, self.used = groups, ahead, 0
        for group in groups[:ahead]:
            for c in group:
                c.start()

    def wait(self):
        for c in self.groups[self.used]:
            c.wait()
        self.used += 1
        after = self.used + self.ahead - 1
        if after < len(self.groups):
            for c in self.groups[after]:
                c.start()


def up_copies(skip, kb, count, wg, wu, wg_held, wu_held, sems):
    groups = []
    for j in range(count):
        at, to = pl.ds(skip + j * kb, kb), pl.ds(j * kb, kb)
        groups.append([
            pltpu.make_async_copy(wg.at[0, at], wg_held.at[to], sems.at[0, j]),
            pltpu.make_async_copy(wu.at[0, at], wu_held.at[to], sems.at[1, j]),
        ])
    return groups


def down_copies(skip, cb, count, wd, held, sems):
    return [[pltpu.make_async_copy(wd.at[0, :, pl.ds(skip + j * cb, cb)], held.at[j], sems.at[j])] for j in range(count)]


def first_kernel(skip, kb, x0, x1, x2, x3, wg, wu, acc, rows, wg_held, wu_held, sems):
    q, width = x0.shape
    hid = wg.shape[2]
    count = width // kb
    stream = Stream(up_copies(skip, kb, count, wg, wu, wg_held, wu_held, sems), FIRST)
    for j in range(count):
        for n, x in enumerate((x0, x1, x2, x3)):
            rows[n * q:(n + 1) * q, :] = x[:, j * kb:(j + 1) * kb]
        stream.wait()
        gate = dot(rows[...], wg_held[j * kb:(j + 1) * kb, :])
        up = dot(rows[...], wu_held[j * kb:(j + 1) * kb, :])
        if j == 0:
            acc[:, :hid] = gate
            acc[:, hid:] = up
        else:
            acc[:, :hid] += gate
            acc[:, hid:] += up


def second_kernel(skip, kb, x0, x1, x2, x3, mask, acc, wg, wu, wd, *rest):
    near, rest = rest[0:4], rest[4:]
    later, rest = rest[0:4], rest[4:]
    rows, total, hidden, scale, wg_held, wu_held, sems, wd_held, wd_sems = rest
    q = x0.shape[0]
    hid = wg.shape[2]
    width = x0.shape[1] - LANES
    count = width // kb
    stream = Stream(
        up_copies(skip, kb, count, wg, wu, wg_held, wu_held, sems)
        + down_copies(0, kb, wd_held.shape[0], wd, wd_held, wd_sems),
        AHEAD,
    )
    for n, x in enumerate((x0, x1, x2, x3)):
        s = jnp.sum(x[:, width:].astype(F32) * mask[...], 1, keepdims=True)
        scale[n * q:(n + 1) * q, :] = jnp.broadcast_to(s, (q, LANES))
    for j in range(count):
        for n, x in enumerate((x0, x1, x2, x3)):
            rows[n * q:(n + 1) * q, :] = x[:, j * kb:(j + 1) * kb]
        stream.wait()
        held = acc if j == 0 else total
        gate = held[:, :hid] + dot(rows[...], wg_held[j * kb:(j + 1) * kb, :])
        up = held[:, hid:] + dot(rows[...], wu_held[j * kb:(j + 1) * kb, :])
        if j < count - 1:
            total[:, :hid] = gate
            total[:, hid:] = up
        else:
            hidden[...] = (gate / (1 + jnp.exp(-gate)) * up).astype(BF16)
    down_blocks(stream, 0, hidden, scale, wd_held, *near)
    down_blocks(stream, near[0].shape[1] // kb, hidden, scale, wd_held, *later)


def down_blocks(stream, base, hidden, scale, held, near, far, near_sent, far_sent):
    q = near.shape[0]
    cb = held.shape[2]
    for j in range(near.shape[1] // cb):
        at = slice(j * cb, (j + 1) * cb)
        stream.wait()
        share = dot(hidden[...], held[base + j]) * scale[:, :1]
        near[:, at] = share[:q]
        far[:, at] = share[q:2 * q]
        near_sent[:, at] = share[2 * q:3 * q].astype(BF16)
        far_sent[:, at] = share[3 * q:].astype(BF16)


def in_vmem(n):
    return [pl.BlockSpec(memory_space=pltpu.VMEM)] * n


def in_hbm(n):
    return [pl.BlockSpec(memory_space=pltpu.HBM)] * n


def params(mib):
    return pltpu.CompilerParams(vmem_limit_bytes=mib << 20)


def first_part(pieces, w_gate, w_up, width, kb):
    q = pieces[0].shape[0]
    hid = w_gate.shape[2]
    return pl.pallas_call(
        functools.partial(first_kernel, 0, kb),
        in_specs=in_vmem(4) + in_hbm(2),
        out_specs=in_vmem(1)[0],
        out_shape=jax.ShapeDtypeStruct((4 * q, 2 * hid), F32),
        scratch_shapes=[pltpu.VMEM((4 * q, kb), BF16)] + held_up(width, hid, kb),
        compiler_params=params(30),
        cost_estimate=cost(WEIGHT * 16 * q * width * hid, WEIGHT * 4 * width * hid),
    )(*pieces, w_gate, w_up)


def second_part(pieces, mask, acc, w_gate, w_up, w_down, skip, down, kb):
    q = pieces[0].shape[0]
    _, full, hid = w_gate.shape
    width = full - skip
    rows = 4 * q
    return pl.pallas_call(
        functools.partial(second_kernel, skip, kb),
        in_specs=in_vmem(6) + in_hbm(3),
        out_specs=in_vmem(8),
        out_shape=shares(q, down) + shares(q, full - down),
        scratch_shapes=[pltpu.VMEM((rows, kb), BF16), pltpu.VMEM((rows, 2 * hid), F32), pltpu.VMEM((rows, hid), BF16), pltpu.VMEM((rows, LANES), F32)]
        + held_up(width, hid, kb) + held_down(full, hid, kb),
        compiler_params=params(SECOND),
        cost_estimate=cost(4 * rows * width * hid + 2 * rows * full * hid, 4 * width * hid + 2 * full * hid),
    )(*pieces, mask, acc, w_gate, w_up, w_down)


def cost(flops, moved):
    return pl.CostEstimate(flops=flops, bytes_accessed=moved, transcendentals=0)


def shares(q, width):
    return [jax.ShapeDtypeStruct((q, width), t) for t in (F32, F32, BF16, BF16)]


def held_up(width, hid, kb):
    return [pltpu.VMEM((width, hid), BF16)] * 2 + [pltpu.SemaphoreType.DMA((2, width // kb))]


def held_down(width, hid, kb):
    return [pltpu.VMEM((width // kb, hid, kb), BF16), pltpu.SemaphoreType.DMA((width // kb,))]


def body(tokens, expert_ids, gate_weights, w_gate, w_up, w_down):
    n_wide = lax.axis_size("wide")
    slices = FF // w_gate.shape[2]
    experts = 2 * n_wide // slices
    expert = lax.axis_index(AXES) // slices
    rows, width = tokens.shape
    plan = exchanges(n_wide)

    named = expert_ids[:, :, None] == jnp.arange(experts, dtype=jnp.int32)[None, None, :]
    table = jnp.sum(jnp.where(named, gate_weights[:, :, None], 0.0), 1)
    extra = jnp.concatenate(split3(table) + [jnp.zeros((rows, LANES - 3 * experts), F32)], 1).astype(BF16)
    lane = jnp.arange(LANES, dtype=jnp.int32)
    mask = ((lane % experts == expert) & (lane < 3 * experts)).astype(F32)[None, :]

    w_gate, w_up, w_down = [pltpu.with_memory_space_constraint(w, pltpu.HBM) for w in (w_gate, w_up, w_down)]
    kb = width // (4 if rows * 2 * n_wide <= 256 else 14)
    cut = CUT * (width // kb) // 14 * kb
    down = DOWN * (width // kb) // 14 * kb
    acc, two = gather(tokens, extra, cut, lambda one: first_part(one, w_gate, w_up, cut, kb), plan)
    pieces = second_part(two, mask, acc, w_gate, w_up, w_down, cut, down, kb)
    core = plan[2]
    far = (pieces[1] + move(pieces[3], core).astype(F32)).astype(BF16)
    out = scatter_sum(pieces[0], pieces[2], far, plan)
    far = (pieces[5] + move(pieces[7], core).astype(F32)).astype(BF16)
    rest = scatter_sum(pieces[4], pieces[6], far, plan)
    return jnp.concatenate([out.astype(BF16), rest.astype(BF16)], 1)


def solution(mesh):
    tokens = P(("group", "wide", "narrow"), None)
    weights = P(("wide", "narrow"), None, None)
    return jax.shard_map(body, mesh=mesh, in_specs=(tokens,) * 3 + (weights,) * 3, out_specs=tokens, check_vma=False)
```

```python
import functools

import jax
import jax.numpy as jnp
from jax import lax
from jax.experimental import pallas as pl
from jax.experimental.pallas import tpu as pltpu
from jax.sharding import PartitionSpec as P

FF = 1024
AXES = ("wide", "narrow")
LANES = 128
CUT = 7
DOWN = 7
AHEAD = 3
FIRST = 5
SECOND = 30
WEIGHT = 20
F32 = jnp.float32
BF16 = jnp.bfloat16


def exchanges(n_wide):
    n = 2 * n_wide
    steps = []
    stride = 8
    rest = n_wide // 4
    while rest > 1:
        radix = min(4, rest)
        steps.append([[(i, i ^ (k * stride)) for i in range(n)] for k in range(1, radix)])
        stride *= radix
        rest //= radix
    steps.append([[(i, i ^ (2 if i % 2 == 0 else 4)) for i in range(n)]])
    last = [(i, i ^ (4 if i % 2 == 0 else 2)) for i in range(n)]
    core = [(i, i ^ 1) for i in range(n)]
    return steps, last, core


def move(x, perm):
    return lax.ppermute(x, AXES, perm)


def after(x, y):
    return lax.optimization_barrier((x, y))


def gather(block, extra, cut, first_product, plan):
    steps, last, core = plan
    for step in steps[:-2]:
        block, extra = [jnp.concatenate([x] + [move(x, p) for p in step], 0) for x in (block, extra)]
    blocks = [block] + [move(block, p) for p in steps[-2]]
    extra, blocks[1] = after(extra, blocks[1])
    extras = [extra] + [move(extra, p) for p in steps[-2]]
    one = jnp.concatenate([x[:, :cut] for x in blocks], 0)
    two = jnp.concatenate([jnp.concatenate([x[:, cut:], e], 1) for x, e in zip(blocks, extras)], 0)
    one, two = [jnp.concatenate([x, move(x, steps[-1][0])], 0) for x in (one, two)]
    other = move(one, last)
    acc = first_product((one, other, move(one, core), move(other, core)))
    other = move(two, last)
    return acc, (two, other, move(two, core), move(other, core))


def scatter_sum(near, near_sent, far, plan):
    steps, last, core = plan
    share = near + move(near_sent, core).astype(F32)
    share = share + move(far, last).astype(F32)
    for step in reversed(steps):
        rows = share.shape[0] // (len(step) + 1)
        got = [move(share[(k + 1) * rows:(k + 2) * rows].astype(BF16), p) for k, p in enumerate(step)]
        share = share[:rows]
        for g in got:
            share = share + g.astype(F32)
    return share


def split3(v):
    high = lax.reduce_precision(v, 8, 7)
    mid = lax.reduce_precision(v - high, 8, 7)
    low = lax.reduce_precision(v - high - mid, 8, 7)
    return [high, mid, low]


def dot(a, b):
    return jnp.dot(a, b, preferred_element_type=F32)


class Stream:
    def __init__(self, groups, ahead):
        self.groups, self.ahead, self.used = groups, ahead, 0
        for group in groups[:ahead]:
            for c in group:
                c.start()

    def wait(self):
        for c in self.groups[self.used]:
            c.wait()
        self.used += 1
        after = self.used + self.ahead - 1
        if after < len(self.groups):
            for c in self.groups[after]:
                c.start()


def up_copies(skip, kb, count, wg, wu, wg_held, wu_held, sems):
    groups = []
    for j in range(count):
        at, to = pl.ds(skip + j * kb, kb), pl.ds(j * kb, kb)
        groups.append([
            pltpu.make_async_copy(wg.at[0, at], wg_held.at[to], sems.at[0, j]),
            pltpu.make_async_copy(wu.at[0, at], wu_held.at[to], sems.at[1, j]),
        ])
    return groups


def down_copies(skip, cb, count, wd, held, sems):
    return [[pltpu.make_async_copy(wd.at[0, :, pl.ds(skip + j * cb, cb)], held.at[j], sems.at[j])] for j in range(count)]


def first_kernel(skip, kb, x0, x1, x2, x3, wg, wu, acc, rows, wg_held, wu_held, sems):
    q, width = x0.shape
    hid = wg.shape[2]
    count = width // kb
    stream = Stream(up_copies(skip, kb, count, wg, wu, wg_held, wu_held, sems), FIRST)
    for j in range(count):
        for n, x in enumerate((x0, x1, x2, x3)):
            rows[n * q:(n + 1) * q, :] = x[:, j * kb:(j + 1) * kb]
        stream.wait()
        gate = dot(rows[...], wg_held[j * kb:(j + 1) * kb, :])
        up = dot(rows[...], wu_held[j * kb:(j + 1) * kb, :])
        if j == 0:
            acc[:, :hid] = gate
            acc[:, hid:] = up
        else:
            acc[:, :hid] += gate
            acc[:, hid:] += up


def second_kernel(skip, kb, x0, x1, x2, x3, mask, acc, wg, wu, wd, *rest):
    near, rest = rest[0:4], rest[4:]
    later, rest = rest[0:4], rest[4:]
    rows, total, hidden, scale, wg_held, wu_held, sems, wd_held, wd_sems = rest
    q = x0.shape[0]
    hid = wg.shape[2]
    width = x0.shape[1] - LANES
    count = width // kb
    stream = Stream(
        up_copies(skip, kb, count, wg, wu, wg_held, wu_held, sems)
        + down_copies(0, kb, wd_held.shape[0], wd, wd_held, wd_sems),
        AHEAD,
    )
    for n, x in enumerate((x0, x1, x2, x3)):
        s = jnp.sum(x[:, width:].astype(F32) * mask[...], 1, keepdims=True)
        scale[n * q:(n + 1) * q, :] = jnp.broadcast_to(s, (q, LANES))
    for j in range(count):
        for n, x in enumerate((x0, x1, x2, x3)):
            rows[n * q:(n + 1) * q, :] = x[:, j * kb:(j + 1) * kb]
        stream.wait()
        held = acc if j == 0 else total
        gate = held[:, :hid] + dot(rows[...], wg_held[j * kb:(j + 1) * kb, :])
        up = held[:, hid:] + dot(rows[...], wu_held[j * kb:(j + 1) * kb, :])
        if j < count - 1:
            total[:, :hid] = gate
            total[:, hid:] = up
        else:
            hidden[...] = (gate / (1 + jnp.exp(-gate)) * up).astype(BF16)
    down_blocks(stream, 0, hidden, scale, wd_held, *near)
    down_blocks(stream, near[0].shape[1] // kb, hidden, scale, wd_held, *later)


def down_blocks(stream, base, hidden, scale, held, near, far, near_sent, far_sent):
    q = near.shape[0]
    cb = held.shape[2]
    for j in range(near.shape[1] // cb):
        at = slice(j * cb, (j + 1) * cb)
        stream.wait()
        share = dot(hidden[...], held[base + j]) * scale[:, :1]
        near[:, at] = share[:q]
        far[:, at] = share[q:2 * q]
        near_sent[:, at] = share[2 * q:3 * q].astype(BF16)
        far_sent[:, at] = share[3 * q:].astype(BF16)


def in_vmem(n):
    return [pl.BlockSpec(memory_space=pltpu.VMEM)] * n


def in_hbm(n):
    return [pl.BlockSpec(memory_space=pltpu.HBM)] * n


def params(mib):
    return pltpu.CompilerParams(vmem_limit_bytes=mib << 20)


def first_part(pieces, w_gate, w_up, width, kb):
    q = pieces[0].shape[0]
    hid = w_gate.shape[2]
    return pl.pallas_call(
        functools.partial(first_kernel, 0, kb),
        in_specs=in_vmem(4) + in_hbm(2),
        out_specs=in_vmem(1)[0],
        out_shape=jax.ShapeDtypeStruct((4 * q, 2 * hid), F32),
        scratch_shapes=[pltpu.VMEM((4 * q, kb), BF16)] + held_up(width, hid, kb),
        compiler_params=params(30),
        cost_estimate=cost(WEIGHT * 16 * q * width * hid, WEIGHT * 4 * width * hid),
    )(*pieces, w_gate, w_up)


def second_part(pieces, mask, acc, w_gate, w_up, w_down, skip, down, kb):
    q = pieces[0].shape[0]
    _, full, hid = w_gate.shape
    width = full - skip
    rows = 4 * q
    return pl.pallas_call(
        functools.partial(second_kernel, skip, kb),
        in_specs=in_vmem(6) + in_hbm(3),
        out_specs=in_vmem(8),
        out_shape=shares(q, down) + shares(q, full - down),
        scratch_shapes=[pltpu.VMEM((rows, kb), BF16), pltpu.VMEM((rows, 2 * hid), F32), pltpu.VMEM((rows, hid), BF16), pltpu.VMEM((rows, LANES), F32)]
        + held_up(width, hid, kb) + held_down(full, hid, kb),
        compiler_params=params(SECOND),
        cost_estimate=cost(4 * rows * width * hid + 2 * rows * full * hid, 4 * width * hid + 2 * full * hid),
    )(*pieces, mask, acc, w_gate, w_up, w_down)


def cost(flops, moved):
    return pl.CostEstimate(flops=flops, bytes_accessed=moved, transcendentals=0)


def shares(q, width):
    return [jax.ShapeDtypeStruct((q, width), t) for t in (F32, F32, BF16, BF16)]


def held_up(width, hid, kb):
    return [pltpu.VMEM((width, hid), BF16)] * 2 + [pltpu.SemaphoreType.DMA((2, width // kb))]


def held_down(width, hid, kb):
    return [pltpu.VMEM((width // kb, hid, kb), BF16), pltpu.SemaphoreType.DMA((width // kb,))]


def body(tokens, expert_ids, gate_weights, w_gate, w_up, w_down):
    n_wide = lax.axis_size("wide")
    slices = FF // w_gate.shape[2]
    experts = 2 * n_wide // slices
    expert = lax.axis_index(AXES) // slices
    rows, width = tokens.shape
    plan = exchanges(n_wide)

    named = expert_ids[:, :, None] == jnp.arange(experts, dtype=jnp.int32)[None, None, :]
    table = jnp.sum(jnp.where(named, gate_weights[:, :, None], 0.0), 1)
    extra = jnp.concatenate(split3(table) + [jnp.zeros((rows, LANES - 3 * experts), F32)], 1).astype(BF16)
    lane = jnp.arange(LANES, dtype=jnp.int32)
    mask = ((lane % experts == expert) & (lane < 3 * experts)).astype(F32)[None, :]

    w_gate, w_up, w_down = [pltpu.with_memory_space_constraint(w, pltpu.HBM) for w in (w_gate, w_up, w_down)]
    kb = width // (4 if rows * 2 * n_wide <= 256 else 14)
    cut = CUT * (width // kb) // 14 * kb
    down = DOWN * (width // kb) // 14 * kb
    acc, two = gather(tokens, extra, cut, lambda one: first_part(one, w_gate, w_up, cut, cut // 7), plan)
    pieces = second_part(two, mask, acc, w_gate, w_up, w_down, cut, down, kb)
    core = plan[2]
    far = (pieces[1] + move(pieces[3], core).astype(F32)).astype(BF16)
    out = scatter_sum(pieces[0], pieces[2], far, plan)
    far = (pieces[5] + move(pieces[7], core).astype(F32)).astype(BF16)
    rest = scatter_sum(pieces[4], pieces[6], far, plan)
    return jnp.concatenate([out.astype(BF16), rest.astype(BF16)], 1)


def solution(mesh):
    tokens = P(("group", "wide", "narrow"), None)
    weights = P(("wide", "narrow"), None, None)
    return jax.shard_map(body, mesh=mesh, in_specs=(tokens,) * 3 + (weights,) * 3, out_specs=tokens, check_vma=False)
```

```python
import functools

import jax
import jax.numpy as jnp
from jax import lax
from jax.experimental import pallas as pl
from jax.experimental.pallas import tpu as pltpu
from jax.sharding import PartitionSpec as P

FF = 1024
AXES = ("wide", "narrow")
LANES = 128
CUT = 7
DOWN = 7
AHEAD = 4
FIRST = 5
SECOND = 30
WEIGHT = 20
F32 = jnp.float32
BF16 = jnp.bfloat16


def exchanges(n_wide):
    n = 2 * n_wide
    steps = []
    stride = 8
    rest = n_wide // 4
    while rest > 1:
        radix = min(4, rest)
        steps.append([[(i, i ^ (k * stride)) for i in range(n)] for k in range(1, radix)])
        stride *= radix
        rest //= radix
    steps.append([[(i, i ^ (2 if i % 2 == 0 else 4)) for i in range(n)]])
    last = [(i, i ^ (4 if i % 2 == 0 else 2)) for i in range(n)]
    core = [(i, i ^ 1) for i in range(n)]
    return steps, last, core


def move(x, perm):
    return lax.ppermute(x, AXES, perm)


def after(x, y):
    return lax.optimization_barrier((x, y))


def gather(block, extra, cut, first_product, plan):
    steps, last, core = plan
    for step in steps[:-2]:
        block, extra = [jnp.concatenate([x] + [move(x, p) for p in step], 0) for x in (block, extra)]
    blocks = [block] + [move(block, p) for p in steps[-2]]
    extra, blocks[1] = after(extra, blocks[1])
    extras = [extra] + [move(extra, p) for p in steps[-2]]
    one = jnp.concatenate([x[:, :cut] for x in blocks], 0)
    two = jnp.concatenate([jnp.concatenate([x[:, cut:], e], 1) for x, e in zip(blocks, extras)], 0)
    one, two = [jnp.concatenate([x, move(x, steps[-1][0])], 0) for x in (one, two)]
    other = move(one, last)
    acc = first_product((one, other, move(one, core), move(other, core)))
    other = move(two, last)
    return acc, (two, other, move(two, core), move(other, core))


def scatter_sum(near, near_sent, far, plan):
    steps, last, core = plan
    share = near + move(near_sent, core).astype(F32)
    share = share + move(far, last).astype(F32)
    for step in reversed(steps):
        rows = share.shape[0] // (len(step) + 1)
        got = [move(share[(k + 1) * rows:(k + 2) * rows].astype(BF16), p) for k, p in enumerate(step)]
        share = share[:rows]
        for g in got:
            share = share + g.astype(F32)
    return share


def split3(v):
    high = lax.reduce_precision(v, 8, 7)
    mid = lax.reduce_precision(v - high, 8, 7)
    low = lax.reduce_precision(v - high - mid, 8, 7)
    return [high, mid, low]


def dot(a, b):
    return jnp.dot(a, b, preferred_element_type=F32)


class Stream:
    def __init__(self, groups, ahead):
        self.groups, self.ahead, self.used = groups, ahead, 0
        for group in groups[:ahead]:
            for c in group:
                c.start()

    def wait(self):
        for c in self.groups[self.used]:
            c.wait()
        self.used += 1
        after = self.used + self.ahead - 1
        if after < len(self.groups):
            for c in self.groups[after]:
                c.start()


def up_copies(skip, kb, count, wg, wu, wg_held, wu_held, sems):
    groups = []
    for j in range(count):
        at, to = pl.ds(skip + j * kb, kb), pl.ds(j * kb, kb)
        groups.append([
            pltpu.make_async_copy(wg.at[0, at], wg_held.at[to], sems.at[0, j]),
            pltpu.make_async_copy(wu.at[0, at], wu_held.at[to], sems.at[1, j]),
        ])
    return groups


def down_copies(skip, cb, count, wd, held, sems):
    return [[pltpu.make_async_copy(wd.at[0, :, pl.ds(skip + j * cb, cb)], held.at[j], sems.at[j])] for j in range(count)]


def first_kernel(skip, kb, x0, x1, x2, x3, wg, wu, acc, rows, wg_held, wu_held, sems):
    q, width = x0.shape
    hid = wg.shape[2]
    count = width // kb
    stream = Stream(up_copies(skip, kb, count, wg, wu, wg_held, wu_held, sems), FIRST)
    for j in range(count):
        for n, x in enumerate((x0, x1, x2, x3)):
            rows[n * q:(n + 1) * q, :] = x[:, j * kb:(j + 1) * kb]
        stream.wait()
        gate = dot(rows[...], wg_held[j * kb:(j + 1) * kb, :])
        up = dot(rows[...], wu_held[j * kb:(j + 1) * kb, :])
        if j == 0:
            acc[:, :hid] = gate
            acc[:, hid:] = up
        else:
            acc[:, :hid] += gate
            acc[:, hid:] += up


def second_kernel(skip, kb, x0, x1, x2, x3, mask, acc, wg, wu, wd, *rest):
    near, rest = rest[0:4], rest[4:]
    later, rest = rest[0:4], rest[4:]
    rows, total, hidden, scale, wg_held, wu_held, sems, wd_held, wd_sems = rest
    q = x0.shape[0]
    hid = wg.shape[2]
    width = x0.shape[1] - LANES
    count = width // kb
    stream = Stream(
        up_copies(skip, kb, count, wg, wu, wg_held, wu_held, sems)
        + down_copies(0, kb, wd_held.shape[0], wd, wd_held, wd_sems),
        AHEAD,
    )
    for n, x in enumerate((x0, x1, x2, x3)):
        s = jnp.sum(x[:, width:].astype(F32) * mask[...], 1, keepdims=True)
        scale[n * q:(n + 1) * q, :] = jnp.broadcast_to(s, (q, LANES))
    for j in range(count):
        for n, x in enumerate((x0, x1, x2, x3)):
            rows[n * q:(n + 1) * q, :] = x[:, j * kb:(j + 1) * kb]
        stream.wait()
        held = acc if j == 0 else total
        gate = held[:, :hid] + dot(rows[...], wg_held[j * kb:(j + 1) * kb, :])
        up = held[:, hid:] + dot(rows[...], wu_held[j * kb:(j + 1) * kb, :])
        if j < count - 1:
            total[:, :hid] = gate
            total[:, hid:] = up
        else:
            hidden[...] = (gate / (1 + jnp.exp(-gate)) * up).astype(BF16)
    down_blocks(stream, 0, hidden, scale, wd_held, *near)
    down_blocks(stream, near[0].shape[1] // kb, hidden, scale, wd_held, *later)


def down_blocks(stream, base, hidden, scale, held, near, far, near_sent, far_sent):
    q = near.shape[0]
    cb = held.shape[2]
    for j in range(near.shape[1] // cb):
        at = slice(j * cb, (j + 1) * cb)
        stream.wait()
        share = dot(hidden[...], held[base + j]) * scale[:, :1]
        near[:, at] = share[:q]
        far[:, at] = share[q:2 * q]
        near_sent[:, at] = share[2 * q:3 * q].astype(BF16)
        far_sent[:, at] = share[3 * q:].astype(BF16)


def in_vmem(n):
    return [pl.BlockSpec(memory_space=pltpu.VMEM)] * n


def in_hbm(n):
    return [pl.BlockSpec(memory_space=pltpu.HBM)] * n


def params(mib):
    return pltpu.CompilerParams(vmem_limit_bytes=mib << 20)


def first_part(pieces, w_gate, w_up, width, kb):
    q = pieces[0].shape[0]
    hid = w_gate.shape[2]
    return pl.pallas_call(
        functools.partial(first_kernel, 0, kb),
        in_specs=in_vmem(4) + in_hbm(2),
        out_specs=in_vmem(1)[0],
        out_shape=jax.ShapeDtypeStruct((4 * q, 2 * hid), F32),
        scratch_shapes=[pltpu.VMEM((4 * q, kb), BF16)] + held_up(width, hid, kb),
        compiler_params=params(30),
        cost_estimate=cost(WEIGHT * 16 * q * width * hid, WEIGHT * 4 * width * hid),
    )(*pieces, w_gate, w_up)


def second_part(pieces, mask, acc, w_gate, w_up, w_down, skip, down, kb):
    q = pieces[0].shape[0]
    _, full, hid = w_gate.shape
    width = full - skip
    rows = 4 * q
    return pl.pallas_call(
        functools.partial(second_kernel, skip, kb),
        in_specs=in_vmem(6) + in_hbm(3),
        out_specs=in_vmem(8),
        out_shape=shares(q, down) + shares(q, full - down),
        scratch_shapes=[pltpu.VMEM((rows, kb), BF16), pltpu.VMEM((rows, 2 * hid), F32), pltpu.VMEM((rows, hid), BF16), pltpu.VMEM((rows, LANES), F32)]
        + held_up(width, hid, kb) + held_down(full, hid, kb),
        compiler_params=params(SECOND),
        cost_estimate=cost(4 * rows * width * hid + 2 * rows * full * hid, 4 * width * hid + 2 * full * hid),
    )(*pieces, mask, acc, w_gate, w_up, w_down)


def cost(flops, moved):
    return pl.CostEstimate(flops=flops, bytes_accessed=moved, transcendentals=0)


def shares(q, width):
    return [jax.ShapeDtypeStruct((q, width), t) for t in (F32, F32, BF16, BF16)]


def held_up(width, hid, kb):
    return [pltpu.VMEM((width, hid), BF16)] * 2 + [pltpu.SemaphoreType.DMA((2, width // kb))]


def held_down(width, hid, kb):
    return [pltpu.VMEM((width // kb, hid, kb), BF16), pltpu.SemaphoreType.DMA((width // kb,))]


def body(tokens, expert_ids, gate_weights, w_gate, w_up, w_down):
    n_wide = lax.axis_size("wide")
    slices = FF // w_gate.shape[2]
    experts = 2 * n_wide // slices
    expert = lax.axis_index(AXES) // slices
    rows, width = tokens.shape
    plan = exchanges(n_wide)

    named = expert_ids[:, :, None] == jnp.arange(experts, dtype=jnp.int32)[None, None, :]
    table = jnp.sum(jnp.where(named, gate_weights[:, :, None], 0.0), 1)
    extra = jnp.concatenate(split3(table) + [jnp.zeros((rows, LANES - 3 * experts), F32)], 1).astype(BF16)
    lane = jnp.arange(LANES, dtype=jnp.int32)
    mask = ((lane % experts == expert) & (lane < 3 * experts)).astype(F32)[None, :]

    w_gate, w_up, w_down = [pltpu.with_memory_space_constraint(w, pltpu.HBM) for w in (w_gate, w_up, w_down)]
    kb = width // (4 if rows * 2 * n_wide <= 256 else 14)
    cut = CUT * (width // kb) // 14 * kb
    down = DOWN * (width // kb) // 14 * kb
    acc, two = gather(tokens, extra, cut, lambda one: first_part(one, w_gate, w_up, cut, cut // 7), plan)
    pieces = second_part(two, mask, acc, w_gate, w_up, w_down, cut, down, kb)
    core = plan[2]
    far = (pieces[1] + move(pieces[3], core).astype(F32)).astype(BF16)
    out = scatter_sum(pieces[0], pieces[2], far, plan)
    far = (pieces[5] + move(pieces[7], core).astype(F32)).astype(BF16)
    rest = scatter_sum(pieces[4], pieces[6], far, plan)
    return jnp.concatenate([out.astype(BF16), rest.astype(BF16)], 1)


def solution(mesh):
    tokens = P(("group", "wide", "narrow"), None)
    weights = P(("wide", "narrow"), None, None)
    return jax.shard_map(body, mesh=mesh, in_specs=(tokens,) * 3 + (weights,) * 3, out_specs=tokens, check_vma=False)
```
